32 devices in a mesh: dp: 4 (over y, x), vocab: 8 (over z, core).
Axes of the slice: x: 2, y: 2, z: 4, core: 2. Of those that a mesh axis runs over, the one named last changes fastest.
Arguments:
- hidden: bfloat16 [256, 4096], P(('dp', 'vocab')), may hold values from -250 to 250
- targets: int32 [256], P(('dp', 'vocab')), may hold values from 0 to 71679, as said below
- loss_weight: bfloat16 [256], P(('dp', 'vocab')), may hold values from 0.5 to 2
- head_weight: bfloat16 [4096, 10240], P(None, 'vocab'), may hold values from -0.09375 to 0.09375
- cluster_weight: bfloat16 [4096, 8], P(None, 'vocab'), may hold values from -0.09375 to 0.09375
- tail_proj: bfloat16 [8, 4096, 1024], P('vocab', None, 'dp'), may hold values from -0.09375 to 0.09375
- tail_out: bfloat16 [8, 1024, 7680], P('vocab', 'dp'), may hold values from -0.1875 to 0.1875
Outputs:
- hidden_grad: bfloat16 [256, 4096], P(('dp', 'vocab'))
- head_grad: bfloat16 [4096, 10240], P('dp', 'vocab')
- cluster_grad: bfloat16 [4096, 8], P('dp', 'vocab')
- proj_grad: bfloat16 [8, 4096, 1024], P('vocab', None, 'dp')
- out_grad: bfloat16 [8, 1024, 7680], P('vocab', 'dp')
The draws below stay inside these ranges and needn't reach their ends.
Inputs may be any that keep to these rules, and one draw needn't show every extreme that they name: In each block of 64 consecutive tokens exactly 32 targets are at or above 10240; at most 16 of them fall in one cluster, and some cluster holds exactly 16 of them in every block.
All inputs are finite; a program needn't handle non-finite values.
Results may differ from the reference program's by a relative error of at most 0.012.
The reference program's roundings to bfloat16 on the way count: a program that leaves them out, or rounds other values in their place, can miss the bound.
Values may be sent and summed in bfloat16 or wider, within the bound.
A program may use at most 128 MiB of HBM per device.

```python
import math
import jax
import jax.numpy as jnp
from jax import lax

MODEL_DIMENSION = 4096
HEAD = 10240
PROJ = 1024
CV = 7680
CLUSTER_TOKEN_CAP = 16
CLUSTERS = 8
TOK_ROW = 64
TOKENS = 256
N_DP = 4


def draw_hidden(key, part):
    base = jax.random.normal(jax.random.fold_in(key, 5), (TOKENS, MODEL_DIMENSION), jnp.float32)
    base = jnp.clip(base, -6.0, 6.0)
    return base.astype(jnp.bfloat16)


def draw_targets(key, part):
    cluster_groups = TOKENS // TOK_ROW
    slots = CLUSTERS * CLUSTER_TOKEN_CAP
    owner = jnp.arange(slots, dtype=jnp.int32) // CLUSTER_TOKEN_CAP

    def one_block(index):
        block_key = jax.random.fold_in(jax.random.fold_in(key, 17), index)
        keys = jax.random.split(block_key, 6)
        heat = jax.random.randint(keys[0], (CLUSTERS,), 0, 4)
        hottest = jax.random.randint(keys[1], (), 0, CLUSTERS)
        noise = jax.random.randint(keys[2], (slots,), 0, 4096)
        score = heat[owner] * 1536 + noise
        score = jnp.where(owner == hottest, 32768, score)
        score = score * slots + jnp.arange(slots, dtype=jnp.int32)
        unused, chosen = lax.top_k(score, TOK_ROW // 2)
        picked = owner[chosen]
        order = jax.random.permutation(keys[3], TOK_ROW)
        cluster = jnp.full((TOK_ROW,), -1, jnp.int32).at[order[:TOK_ROW // 2]].set(picked)
        head_word = jax.random.randint(keys[4], (TOK_ROW,), 0, HEAD)
        tail_word = jax.random.randint(keys[5], (TOK_ROW,), 0, CV)
        return jnp.where(cluster < 0, head_word, HEAD + cluster * CV + tail_word)
    return jax.vmap(one_block)(jnp.arange(cluster_groups)).reshape(TOKENS).astype(jnp.int32)


def block_scale(stream_key, extent, pieces, low, high):
    def one(position, shards_of):
        heights = jax.random.uniform(jax.random.fold_in(jax.random.fold_in(stream_key, 6), position), (shards_of,), jnp.float32, low / len(pieces), high / len(pieces))
        return jnp.repeat(jnp.exp(heights), extent[position] // shards_of).reshape((-1,) + (1,) * (len(extent) - position - 1))

    level = one(*pieces[0])
    for cut in pieces[1:]:
        level = level * one(*cut)
    return level


def centred(stream_key, shape, scale, limit, shards=(), held_as=jnp.bfloat16):
    level = block_scale(stream_key, shape, shards, -0.22, 0.18) if shards else 1.0
    result = jax.random.normal(stream_key, shape, jnp.float32) * scale * level
    return jnp.minimum(jnp.maximum(result, -limit), limit).astype(held_as)


def setup_inputs(seed: int = 0) -> dict:
    splits = jax.random.split(jax.random.key(seed), 8)
    hidden = draw_hidden(jax.random.fold_in(splits[7], 71), 0)
    targets = draw_targets(jax.random.fold_in(splits[7], 71), 0)
    loss_weight = jnp.clip(jnp.exp(math.log(2.0) - 1.3862944 * jax.random.uniform(splits[2], (TOKENS,), jnp.float32) ** block_scale(splits[2], (TOKENS,), ((0, 32),), -0.2, 0.2)), 0.5, 2.0).astype(jnp.bfloat16)
    head_weight = centred(splits[3], (MODEL_DIMENSION, HEAD), MODEL_DIMENSION ** -0.5, 0.09375, ((1, 8),))
    cluster_weight = centred(splits[4], (MODEL_DIMENSION, CLUSTERS), MODEL_DIMENSION ** -0.5, 0.09375, ((1, 8),))
    tail_proj = centred(splits[5], (CLUSTERS, MODEL_DIMENSION, PROJ), MODEL_DIMENSION ** -0.5, 0.09375, ((0, 8), (2, 4)))
    tail_out = centred(splits[6], (CLUSTERS, PROJ, CV), PROJ ** -0.5, 0.1875, ((0, 8), (1, 4)))
    return dict(hidden=hidden, targets=targets, loss_weight=loss_weight, head_weight=head_weight, cluster_weight=cluster_weight, tail_proj=tail_proj, tail_out=tail_out)


def pick_rows(hidden_block_list, target_blocks, weight_blocks, cluster):
    offset = target_blocks - HEAD
    member = (offset >= 0) & (offset // CV == cluster)
    rank = jnp.cumsum(member.astype(jnp.int32), axis=1) - 1
    slots = jnp.arange(CLUSTER_TOKEN_CAP, dtype=jnp.int32)
    select = member[:, None, :] & (rank[:, None, :] == slots[None, :, None])
    cluster_selector = select.astype(jnp.float32)
    token_row_list = jnp.einsum("ahw,awo->aho", cluster_selector, hidden_block_list.astype(jnp.float32), precision=lax.Precision.HIGHEST)
    words = jnp.sum(jnp.where(select, (offset % CV)[:, None, :], 0), axis=2).astype(jnp.int32)
    gains = jnp.sum(jnp.where(select, weight_blocks.astype(jnp.float32)[:, None, :], 0.0), axis=2)
    return token_row_list.astype(jnp.bfloat16), words, gains, cluster_selector


def reference(hidden, targets, loss_weight, head_weight, cluster_weight, tail_proj, tail_out):
    gain = loss_weight.astype(jnp.float32)
    every_weight = jnp.concatenate([head_weight, cluster_weight], axis=1)
    logits = jnp.dot(hidden, every_weight, preferred_element_type=jnp.float32)
    offset = targets - HEAD
    target_column = jnp.where(offset >= 0, HEAD + offset // CV, targets).astype(jnp.int32)
    top = jnp.max(logits, axis=1, keepdims=True)
    expo = jnp.exp(logits - top)
    prob = expo / jnp.sum(expo, axis=1, keepdims=True)
    columns = jnp.arange(logits.shape[1], dtype=jnp.int32)
    onehot = (columns[None, :] == target_column[:, None]).astype(jnp.float32)
    delta = (gain[:, None] * (prob - onehot)).astype(jnp.bfloat16)
    head_part = lax.dot_general(delta, every_weight, (((1,), (1,)), ((), ())), preferred_element_type=jnp.float32)
    weight_grad = lax.dot_general(hidden, delta, (((0,), (0,)), ((), ())), preferred_element_type=jnp.float32).astype(jnp.bfloat16)
    cluster_groups = N_DP
    span = TOKENS // N_DP
    hidden_block_list = hidden.reshape(cluster_groups, span, MODEL_DIMENSION)
    target_blocks = targets.reshape(cluster_groups, span)
    weight_blocks = loss_weight.reshape(cluster_groups, span)
    word_columns = jnp.arange(CV, dtype=jnp.int32)

    def one_cluster(carry, inputs):
        cluster, proj, out = inputs
        token_row_list, words, gains, cluster_selector = pick_rows(hidden_block_list, target_blocks, weight_blocks, cluster)
        token_row_list = token_row_list.reshape(cluster_groups * CLUSTER_TOKEN_CAP, MODEL_DIMENSION)
        words = words.reshape(cluster_groups * CLUSTER_TOKEN_CAP)
        gains = gains.reshape(cluster_groups * CLUSTER_TOKEN_CAP)
        reduced = jnp.dot(token_row_list, proj, preferred_element_type=jnp.float32).astype(jnp.bfloat16)
        word_logits = jnp.dot(reduced, out, preferred_element_type=jnp.float32)
        word_top = jnp.max(word_logits, axis=1, keepdims=True)
        word_exp = jnp.exp(word_logits - word_top)
        word_prob = word_exp / jnp.sum(word_exp, axis=1, keepdims=True)
        word_hot = (word_columns[None, :] == words[:, None]).astype(jnp.float32)
        word_delta = (gains[:, None] * (word_prob - word_hot)).astype(jnp.bfloat16)
        reduced_grad = lax.dot_general(word_delta, out, (((1,), (1,)), ((), ())), preferred_element_type=jnp.float32).astype(jnp.bfloat16)
        out_grad = lax.dot_general(reduced, word_delta, (((0,), (0,)), ((), ())), preferred_element_type=jnp.float32).astype(jnp.bfloat16)
        proj_grad = lax.dot_general(token_row_list, reduced_grad, (((0,), (0,)), ((), ())), preferred_element_type=jnp.float32).astype(jnp.bfloat16)
        tail_portion = lax.dot_general(reduced_grad, proj, (((1,), (1,)), ((), ())), preferred_element_type=jnp.float32)
        backward_result = jnp.einsum("vpg,vpl->vgl", cluster_selector, tail_portion.reshape(cluster_groups, CLUSTER_TOKEN_CAP, MODEL_DIMENSION), precision=lax.Precision.HIGHEST)
        return carry + backward_result, (proj_grad, out_grad)

    start = jnp.zeros((cluster_groups, span, MODEL_DIMENSION), jnp.float32)
    cluster_ids = jnp.arange(CLUSTERS, dtype=jnp.int32)
    tail_back, grads = lax.scan(one_cluster, start, (cluster_ids, tail_proj, tail_out))
    proj_grad, out_grad = grads
    hidden_grad = (head_part + tail_back.reshape(TOKENS, MODEL_DIMENSION)).astype(jnp.bfloat16)
    return hidden_grad, weight_grad[:, :HEAD], weight_grad[:, HEAD:], proj_grad, out_grad
```

```python
import jax
import jax.numpy as jnp
from jax import lax
from jax.sharding import PartitionSpec as P

HEAD = 10240
CV = 7680
CLUSTER_TOKEN_CAP = 16


def shards(hidden, targets, loss_weight, head_weight, cluster_weight, tail_proj, tail_out):
    vocab_index = lax.axis_index("vocab")
    dp_index = lax.axis_index("dp")
    n_dp = lax.axis_size("dp")
    n_vocab = lax.axis_size("vocab")
    local, model = hidden.shape
    span = local * n_vocab
    share = model // n_dp
    cap = CLUSTER_TOKEN_CAP
    f32, bf16 = jnp.float32, jnp.bfloat16

    facts = lax.all_gather(
        jnp.stack([targets.astype(f32), loss_weight.astype(f32)]),
        ("dp", "vocab"), axis=1, tiled=True,
    )
    all_targets = facts[0].astype(jnp.int32)
    all_weights = facts[1]
    all_hidden = lax.all_gather(hidden, ("dp", "vocab"), axis=0, tiled=True)
    rows_hidden = lax.dynamic_slice_in_dim(all_hidden, dp_index * span, span, 0)
    row_targets = lax.dynamic_slice_in_dim(all_targets, dp_index * span, span, 0)
    gain_rows = lax.dynamic_slice_in_dim(all_weights, dp_index * span, span, 0)

    blocks = all_targets.reshape(n_dp, span)
    offset = blocks - HEAD
    member = (offset >= 0) & (offset // CV == vocab_index)
    place = jnp.arange(span, dtype=jnp.int32)
    rank = jnp.sum(
        (member[:, None, :] & (place[None, None, :] < place[None, :, None])).astype(jnp.int32), axis=2
    )
    slots = jnp.arange(cap, dtype=jnp.int32)
    select = member[:, None, :] & (rank[:, None, :] == slots[None, :, None])
    own_select = lax.dynamic_index_in_dim(select, dp_index, 0, False)
    own_words = jnp.sum(
        jnp.where(own_select, (row_targets - HEAD)[None, :] % CV, 0), axis=1
    ).astype(jnp.int32)
    own_gains = jnp.sum(jnp.where(own_select, gain_rows[None, :], 0.0), axis=1)
    tail_rows = jnp.einsum(
        "ahw,awo->aho", select.astype(bf16), all_hidden.reshape(n_dp, span, model),
        preferred_element_type=f32,
    ).astype(bf16).reshape(n_dp * cap, model)

    proj = tail_proj[0]
    out = tail_out[0]
    reduced = jnp.dot(tail_rows, proj, preferred_element_type=f32).astype(bf16)
    partial_logits = jnp.dot(reduced, out, preferred_element_type=f32)
    word_logits = lax.psum_scatter(partial_logits, "dp", scatter_dimension=0, tiled=True)

    local_logits = jnp.dot(rows_hidden, head_weight, preferred_element_type=f32)
    cluster_logit = jnp.dot(rows_hidden, cluster_weight, preferred_element_type=f32)
    width = head_weight.shape[1]
    columns = vocab_index * width + jnp.arange(width, dtype=jnp.int32)
    row_offset = row_targets - HEAD
    target_column = jnp.where(row_offset >= 0, HEAD + row_offset // CV, row_targets)
    top = jnp.maximum(jnp.max(local_logits, axis=1), cluster_logit[:, 0])
    total = jnp.sum(jnp.exp(local_logits - top[:, None]), axis=1) + jnp.exp(cluster_logit[:, 0] - top)
    stats = lax.all_gather(jnp.stack([top, total]), "vocab")
    top = jnp.max(stats[:, 0], axis=0)
    total = jnp.sum(stats[:, 1] * jnp.exp(stats[:, 0] - top[None, :]), axis=0)
    head_hot = (columns[None, :] == target_column[:, None]).astype(f32)
    head_delta = (
        gain_rows[:, None] * (jnp.exp(local_logits - top[:, None]) / total[:, None] - head_hot)
    ).astype(bf16)
    cluster_hot = (target_column == HEAD + vocab_index).astype(f32)[:, None]
    cluster_delta = (
        gain_rows[:, None] * (jnp.exp(cluster_logit - top[:, None]) / total[:, None] - cluster_hot)
    ).astype(bf16)
    all_delta = lax.all_gather(head_delta, "dp", axis=0, tiled=True)
    all_cluster_delta = lax.all_gather(cluster_delta, "dp", axis=0, tiled=True)
    token_partial = lax.dot_general(
        head_delta, head_weight, (((1,), (1,)), ((), ())), preferred_element_type=f32
    ) + cluster_delta.astype(f32) * cluster_weight.astype(f32).T

    word_top = jnp.max(word_logits, axis=1, keepdims=True)
    word_exp = jnp.exp(word_logits - word_top)
    word_prob = word_exp / jnp.sum(word_exp, axis=1, keepdims=True)
    word_columns = jnp.arange(word_logits.shape[1], dtype=jnp.int32)
    word_hot = (word_columns[None, :] == own_words[:, None]).astype(f32)
    own_word_delta = (own_gains[:, None] * (word_prob - word_hot)).astype(bf16)
    word_delta = lax.all_gather(own_word_delta, "dp", axis=0, tiled=True)
    reduced_grad = lax.dot_general(
        word_delta, out, (((1,), (1,)), ((), ())), preferred_element_type=f32
    ).astype(bf16)
    tail_partial = lax.dot_general(
        reduced_grad, proj, (((1,), (1,)), ((), ())), preferred_element_type=f32
    )
    tail_sum = lax.psum_scatter(
        tail_partial.astype(bf16), "dp", scatter_dimension=0, tiled=True
    )
    out_grad = lax.dot_general(
        reduced, word_delta, (((0,), (0,)), ((), ())), preferred_element_type=f32
    ).astype(bf16)
    proj_grad = lax.dot_general(
        tail_rows, reduced_grad, (((0,), (0,)), ((), ())), preferred_element_type=f32
    ).astype(bf16)

    hidden_columns = lax.dynamic_slice_in_dim(all_hidden, dp_index * share, share, 1)
    head_grad = lax.dot_general(
        hidden_columns, all_delta, (((0,), (0,)), ((), ())), preferred_element_type=f32
    ).astype(bf16)
    cluster_grad = lax.dot_general(
        hidden_columns, all_cluster_delta, (((0,), (0,)), ((), ())), preferred_element_type=f32
    ).astype(bf16)

    spread_back = lax.dot_general(
        own_select.astype(bf16), tail_sum, (((0,), (0,)), ((), ())), preferred_element_type=f32
    )
    hidden_grad = lax.psum_scatter(
        token_partial + spread_back, "vocab", scatter_dimension=0, tiled=True
    ).astype(bf16)
    return (hidden_grad, head_grad, cluster_grad, proj_grad[None], out_grad[None])


def solution(mesh):
    placed = (
        P(("dp", "vocab"), None),
        P(("dp", "vocab")),
        P(("dp", "vocab")),
        P(None, "vocab"),
        P(None, "vocab"),
        P("vocab", None, "dp"),
        P("vocab", "dp", None),
    )
    return jax.shard_map(
        shards,
        mesh=mesh,
        in_specs=placed,
        out_specs=(
            P(("dp", "vocab"), None),
            P("dp", "vocab"),
            P("dp", "vocab"),
            P("vocab", None, "dp"),
            P("vocab", "dp", None),
        ),
        check_vma=False,
    )
```

```python
import functools

import jax
import jax.numpy as jnp
from jax import lax
from jax.experimental import pallas as pl
from jax.experimental.pallas import tpu as pltpu
from jax.sharding import PartitionSpec as P

HEAD = 10240
CV = 7680
CLUSTER_TOKEN_CAP = 16
MESH = pl.DeviceIdType.MESH
VMEM_LIMIT = 56 * 2**20


def remote(src, dst, send, recv, axis, peer):
    return pltpu.make_async_remote_copy(
        src_ref=src, dst_ref=dst, send_sem=send, recv_sem=recv,
        device_id={axis: peer}, device_id_type=MESH,
    )


def greet(axis, peers):
    barrier = pltpu.get_barrier_semaphore()
    for peer in peers:
        pl.semaphore_signal(barrier, inc=1, device_id={axis: peer}, device_id_type=MESH)
    pl.semaphore_wait(barrier, len(peers))


def call(body, operands, results, scratch, collective_id):
    vmem = pl.BlockSpec(memory_space=pltpu.VMEM)
    return pl.pallas_call(
        body,
        out_shape=results,
        in_specs=[vmem] * len(operands),
        out_specs=[vmem] * len(results),
        scratch_shapes=scratch,
        compiler_params=pltpu.CompilerParams(
            collective_id=collective_id, has_side_effects=True, vmem_limit_bytes=VMEM_LIMIT
        ),
    )(*operands)


def exchange_body(axis, n, split, count, *refs):
    ins, outs = refs[:count], refs[count : 2 * count]
    send, recv, local = refs[2 * count :]
    me = lax.axis_index(axis)
    peers = [lax.rem(me + k, n) for k in range(1, n)]
    greet(axis, peers)
    copies = []
    for i in range(count):
        for k, peer in enumerate(peers):
            src = ins[i].at[peer] if split[i] else ins[i]
            copy = remote(src, outs[i].at[me], send.at[i, k], recv.at[i, k], axis, peer)
            copy.start()
            copies.append(copy)
    for i in range(count):
        src = ins[i].at[me] if split[i] else ins[i]
        copy = pltpu.make_async_copy(src, outs[i].at[me], local.at[i])
        copy.start()
        copies.append(copy)
    for copy in copies:
        copy.wait()


def exchange(axis, gathers, splits, collective_id):
    n = lax.axis_size(axis)
    operands = [*gathers, *splits]
    count = len(operands)
    results = [jax.ShapeDtypeStruct((n, *a.shape), a.dtype) for a in gathers]
    results += [jax.ShapeDtypeStruct(a.shape, a.dtype) for a in splits]
    split = [False] * len(gathers) + [True] * len(splits)
    dma = pltpu.SemaphoreType.DMA
    return call(
        functools.partial(exchange_body, axis, n, split, count),
        operands, results,
        [dma((count, n - 1)), dma((count, n - 1)), dma((count,))],
        collective_id,
    )


def pair_gather_body(axis, n, count, *refs):
    ins, outs = refs[:count], refs[count : 2 * count]
    send, recv, pass_send, pass_recv, local = refs[2 * count :]
    half = n // 2
    me = lax.axis_index(axis)
    place, core = me // 2, lax.rem(me, 2)
    partner = 2 * place + 1 - core
    peers = [2 * lax.rem(place + k, half) + core for k in range(1, half)]
    greet(axis, peers + [partner])
    copies, passed = [], []
    for i in range(count):
        for k, peer in enumerate(peers):
            copy = remote(ins[i], outs[i].at[me], send.at[i, k], recv.at[i, k], axis, peer)
            copy.start()
            copies.append(copy)
        copy = remote(ins[i], outs[i].at[me], pass_send.at[i, 0], pass_recv.at[i, 0], axis, partner)
        copy.start()
        passed.append(copy)
        copy = pltpu.make_async_copy(ins[i], outs[i].at[me], local.at[i])
        copy.start()
        passed.append(copy)
    for k in range(1, half):
        source = 2 * lax.rem(place + half - k, half) + core
        for i in range(count):
            copies[i * (half - 1) + k - 1].wait_recv()
            block = outs[i].at[source]
            copy = remote(block, block, pass_send.at[i, k], pass_recv.at[i, k], axis, partner)
            copy.start()
            passed.append(copy)
    for copy in copies:
        copy.wait_send()
    for copy in passed:
        copy.wait()


def pair_gather(axis, operands, collective_id):
    n = lax.axis_size(axis)
    count = len(operands)
    dma = pltpu.SemaphoreType.DMA
    half = n // 2
    return call(
        functools.partial(pair_gather_body, axis, n, count),
        operands,
        [jax.ShapeDtypeStruct((n, *a.shape), a.dtype) for a in operands],
        [dma((count, half - 1)), dma((count, half - 1)), dma((count, half)), dma((count, half)), dma((count,))],
        collective_id,
    )


def pair_scatter_body(axis, n, x, out, theirs, mine, landed, send, recv, pair_send, pair_recv):
    half = n // 2
    me = lax.axis_index(axis)
    place, core = me // 2, lax.rem(me, 2)
    partner = 2 * place + 1 - core
    order = [lax.rem(place + k, half) for k in range(1, half)]
    greet(axis, [2 * p + core for p in order] + [partner])
    order = order + [place]
    pairs, copies = [], []
    for k, p in enumerate(order):
        copy = remote(x.at[2 * p + 1 - core], theirs.at[k], pair_send.at[k], pair_recv.at[k], axis, partner)
        copy.start()
        pairs.append(copy)
    for k, p in enumerate(order):
        pairs[k].wait_recv()
        mine[k] = x[2 * p + core] + theirs[k]
        if k < half - 1:
            copy = remote(mine.at[k], landed.at[k], send.at[k], recv.at[k], axis, 2 * p + core)
            copy.start()
            copies.append(copy)
    total = mine[half - 1]
    for k, copy in enumerate(copies):
        copy.wait_recv()
        total = total + landed[k]
    out[...] = total
    for copy in pairs + copies:
        copy.wait_send()


def pair_scatter(axis, x, collective_id):
    n = lax.axis_size(axis)
    half = n // 2
    block = x.shape[1:]
    dma = pltpu.SemaphoreType.DMA
    return call(
        functools.partial(pair_scatter_body, axis, n),
        [x], [jax.ShapeDtypeStruct(block, x.dtype)],
        [
            pltpu.VMEM((half, *block), x.dtype),
            pltpu.VMEM((half, *block), x.dtype),
            pltpu.VMEM((half - 1, *block), x.dtype),
            dma((half - 1,)), dma((half - 1,)), dma((half,)), dma((half,)),
        ],
        collective_id,
    )[0]


def lanes(rows):
    x = jnp.stack([r.astype(jnp.float32) for r in rows])
    return jnp.pad(x, ((0, -x.shape[0] % 8), (0, -x.shape[1] % 128)))


def shards(hidden, targets, loss_weight, head_weight, cluster_weight, tail_proj, tail_out):
    vocab_index = lax.axis_index("vocab")
    n_dp = lax.axis_size("dp")
    n_vocab = lax.axis_size("vocab")
    local, model = hidden.shape
    span = local * n_vocab
    share = model // n_dp
    cap = CLUSTER_TOKEN_CAP
    f32, bf16 = jnp.float32, jnp.bfloat16

    held, facts = pair_gather(
        "vocab", [hidden.reshape(2 * local, model // 2), lanes([targets, loss_weight])], 1
    )
    rows_hidden = held.reshape(span, model)
    row_targets = facts[:, 0, :local].reshape(span).astype(jnp.int32)
    gain_rows = facts[:, 1, :local].reshape(span)

    offset = row_targets - HEAD
    member = (offset >= 0) & (offset // CV == vocab_index)
    place = jnp.arange(span, dtype=jnp.int32)
    rank = jnp.sum((member[None, :] & (place[None, :] < place[:, None])).astype(jnp.int32), axis=1)
    slots = jnp.arange(cap, dtype=jnp.int32)
    own_select = member[None, :] & (rank[None, :] == slots[:, None])
    own_words = jnp.sum(jnp.where(own_select, offset[None, :] % CV, 0), axis=1).astype(jnp.int32)
    own_gains = jnp.sum(jnp.where(own_select, gain_rows[None, :], 0.0), axis=1)
    own_rows = jnp.dot(own_select.astype(bf16), rows_hidden, preferred_element_type=f32).astype(bf16)
    pieces = rows_hidden.reshape(span, n_dp, share).transpose(1, 0, 2)
    tail_rows, hidden_columns = exchange("dp", [own_rows], [pieces], 2)
    tail_rows = tail_rows.reshape(n_dp * cap, model)
    hidden_columns = hidden_columns.reshape(n_dp * span, share)

    proj = tail_proj[0]
    out = tail_out[0]
    reduced = jnp.dot(tail_rows, proj, preferred_element_type=f32).astype(bf16)
    partial_logits = jnp.dot(reduced, out, preferred_element_type=f32)
    word_logits = lax.psum_scatter(partial_logits, "dp", scatter_dimension=0, tiled=True)

    local_logits = jnp.dot(rows_hidden, head_weight, preferred_element_type=f32)
    cluster_logit = jnp.dot(rows_hidden, cluster_weight, preferred_element_type=f32)
    width = head_weight.shape[1]
    columns = vocab_index * width + jnp.arange(width, dtype=jnp.int32)
    row_offset = row_targets - HEAD
    target_column = jnp.where(row_offset >= 0, HEAD + row_offset // CV, row_targets)
    top = jnp.maximum(jnp.max(local_logits, axis=1), cluster_logit[:, 0])
    total = jnp.sum(jnp.exp(local_logits - top[:, None]), axis=1) + jnp.exp(cluster_logit[:, 0] - top)
    (stats,) = exchange("vocab", [lanes([top, total])], [], 3)
    tops, totals = stats[:, 0, :span], stats[:, 1, :span]
    top = jnp.max(tops, axis=0)
    total = jnp.sum(totals * jnp.exp(tops - top[None, :]), axis=0)
    head_hot = (columns[None, :] == target_column[:, None]).astype(f32)
    head_delta = (
        gain_rows[:, None] * (jnp.exp(local_logits - top[:, None]) / total[:, None] - head_hot)
    ).astype(bf16)
    cluster_hot = (target_column == HEAD + vocab_index).astype(f32)[:, None]
    cluster_delta = (
        gain_rows[:, None] * (jnp.exp(cluster_logit - top[:, None]) / total[:, None] - cluster_hot)
    ).astype(bf16)
    token_partial = lax.dot_general(
        head_delta, head_weight, (((1,), (1,)), ((), ())), preferred_element_type=f32
    ) + cluster_delta.astype(f32) * cluster_weight.astype(f32).T

    word_top = jnp.max(word_logits, axis=1, keepdims=True)
    word_exp = jnp.exp(word_logits - word_top)
    word_prob = word_exp / jnp.sum(word_exp, axis=1, keepdims=True)
    word_columns = jnp.arange(word_logits.shape[1], dtype=jnp.int32)
    word_hot = (word_columns[None, :] == own_words[:, None]).astype(f32)
    own_word_delta = (own_gains[:, None] * (word_prob - word_hot)).astype(bf16)
    deltas = jnp.concatenate([head_delta, cluster_delta], axis=1)
    deltas = jnp.pad(deltas, ((0, 0), (0, -deltas.shape[1] % 128)))
    word_delta, deltas = exchange("dp", [own_word_delta, deltas], [], 4)
    word_delta = word_delta.reshape(n_dp * cap, -1)
    deltas = deltas.reshape(n_dp * span, -1)
    all_delta, all_cluster_delta = deltas[:, :width], deltas[:, width : width + 1]
    reduced_grad = lax.dot_general(
        word_delta, out, (((1,), (1,)), ((), ())), preferred_element_type=f32
    ).astype(bf16)
    tail_partial = lax.dot_general(
        reduced_grad, proj, (((1,), (1,)), ((), ())), preferred_element_type=f32
    )
    (tail_parts,) = exchange("dp", [], [tail_partial.astype(bf16).reshape(n_dp, cap, model)], 5)
    tail_sum = jnp.sum(tail_parts.astype(f32), axis=0).astype(bf16)
    out_grad = lax.dot_general(
        reduced, word_delta, (((0,), (0,)), ((), ())), preferred_element_type=f32
    ).astype(bf16)
    proj_grad = lax.dot_general(
        tail_rows, reduced_grad, (((0,), (0,)), ((), ())), preferred_element_type=f32
    ).astype(bf16)

    head_grad = lax.dot_general(
        hidden_columns, all_delta, (((0,), (0,)), ((), ())), preferred_element_type=f32
    ).astype(bf16)
    cluster_grad = lax.dot_general(
        hidden_columns, all_cluster_delta, (((0,), (0,)), ((), ())), preferred_element_type=f32
    ).astype(bf16)

    spread_back = lax.dot_general(
        own_select.astype(bf16), tail_sum, (((0,), (0,)), ((), ())), preferred_element_type=f32
    )
    partial = (token_partial + spread_back).reshape(n_vocab, local, model)
    hidden_grad = pair_scatter("vocab", partial, 6).astype(bf16)
    return (hidden_grad, head_grad, cluster_grad, proj_grad[None], out_grad[None])


def solution(mesh):
    placed = (
        P(("dp", "vocab"), None),
        P(("dp", "vocab")),
        P(("dp", "vocab")),
        P(None, "vocab"),
        P(None, "vocab"),
        P("vocab", None, "dp"),
        P("vocab", "dp", None),
    )
    return jax.shard_map(
        shards,
        mesh=mesh,
        in_specs=placed,
        out_specs=(
            P(("dp", "vocab"), None),
            P("dp", "vocab"),
            P("dp", "vocab"),
            P("vocab", None, "dp"),
            P("vocab", "dp", None),
        ),
        check_vma=False,
    )
```

```python
import functools

import jax
import jax.numpy as jnp
from jax import lax
from jax.experimental import pallas as pl
from jax.experimental.pallas import tpu as pltpu
from jax.sharding import PartitionSpec as P

HEAD = 10240
CV = 7680
CLUSTER_TOKEN_CAP = 16
MESH = pl.DeviceIdType.MESH
VMEM_LIMIT = 56 * 2**20


def remote(src, dst, send, recv, axis, peer):
    return pltpu.make_async_remote_copy(
        src_ref=src, dst_ref=dst, send_sem=send, recv_sem=recv,
        device_id={axis: peer}, device_id_type=MESH,
    )


def greet(axis, peers):
    barrier = pltpu.get_barrier_semaphore()
    for peer in peers:
        pl.semaphore_signal(barrier, inc=1, device_id={axis: peer}, device_id_type=MESH)
    pl.semaphore_wait(barrier, len(peers))


def call(body, operands, results, scratch, collective_id):
    vmem = pl.BlockSpec(memory_space=pltpu.VMEM)
    return pl.pallas_call(
        body,
        out_shape=results,
        in_specs=[vmem] * len(operands),
        out_specs=[vmem] * len(results),
        scratch_shapes=scratch,
        compiler_params=pltpu.CompilerParams(
            collective_id=collective_id, has_side_effects=True, vmem_limit_bytes=VMEM_LIMIT
        ),
    )(*operands)


def exchange_body(axis, n, split, count, *refs):
    ins, outs = refs[:count], refs[count : 2 * count]
    send, recv, local = refs[2 * count :]
    me = lax.axis_index(axis)
    peers = [lax.rem(me + k, n) for k in range(1, n)]
    greet(axis, peers)
    copies = []
    for i in range(count):
        for k, peer in enumerate(peers):
            src = ins[i].at[peer] if split[i] else ins[i]
            copy = remote(src, outs[i].at[me], send.at[i, k], recv.at[i, k], axis, peer)
            copy.start()
            copies.append(copy)
    for i in range(count):
        src = ins[i].at[me] if split[i] else ins[i]
        copy = pltpu.make_async_copy(src, outs[i].at[me], local.at[i])
        copy.start()
        copies.append(copy)
    for copy in copies:
        copy.wait()


def exchange(axis, gathers, splits, collective_id):
    n = lax.axis_size(axis)
    operands = [*gathers, *splits]
    count = len(operands)
    results = [jax.ShapeDtypeStruct((n, *a.shape), a.dtype) for a in gathers]
    results += [jax.ShapeDtypeStruct(a.shape, a.dtype) for a in splits]
    split = [False] * len(gathers) + [True] * len(splits)
    dma = pltpu.SemaphoreType.DMA
    return call(
        functools.partial(exchange_body, axis, n, split, count),
        operands, results,
        [dma((count, n - 1)), dma((count, n - 1)), dma((count,))],
        collective_id,
    )


def pair_gather_body(axis, n, count, *refs):
    ins, outs = refs[:count], refs[count : 2 * count]
    send, recv, pass_send, pass_recv, local = refs[2 * count :]
    half = n // 2
    me = lax.axis_index(axis)
    place, core = me // 2, lax.rem(me, 2)
    partner = 2 * place + 1 - core
    peers = [2 * lax.rem(place + k, half) + core for k in range(1, half)]
    greet(axis, peers + [partner])
    copies, passed = [], []
    for i in range(count):
        for k, peer in enumerate(peers):
            copy = remote(ins[i], outs[i].at[me], send.at[i, k], recv.at[i, k], axis, peer)
            copy.start()
            copies.append(copy)
        copy = remote(ins[i], outs[i].at[me], pass_send.at[i, 0], pass_recv.at[i, 0], axis, partner)
        copy.start()
        passed.append(copy)
        copy = pltpu.make_async_copy(ins[i], outs[i].at[me], local.at[i])
        copy.start()
        passed.append(copy)
    for k in range(1, half):
        source = 2 * lax.rem(place + half - k, half) + core
        for i in range(count):
            copies[i * (half - 1) + k - 1].wait_recv()
            block = outs[i].at[source]
            copy = remote(block, block, pass_send.at[i, k], pass_recv.at[i, k], axis, partner)
            copy.start()
            passed.append(copy)
    for copy in copies:
        copy.wait_send()
    for copy in passed:
        copy.wait()


def pair_gather(axis, operands, collective_id):
    n = lax.axis_size(axis)
    count = len(operands)
    dma = pltpu.SemaphoreType.DMA
    half = n // 2
    return call(
        functools.partial(pair_gather_body, axis, n, count),
        operands,
        [jax.ShapeDtypeStruct((n, *a.shape), a.dtype) for a in operands],
        [dma((count, half - 1)), dma((count, half - 1)), dma((count, half)), dma((count, half)), dma((count,))],
        collective_id,
    )


def pair_scatter_body(axis, n, x, out, theirs, leaving, landed, send, recv, pair_send, pair_recv):
    half = n // 2
    me = lax.axis_index(axis)
    place, core = me // 2, lax.rem(me, 2)
    partner = 2 * place + 1 - core
    order = [lax.rem(place + k, half) for k in range(1, half)]
    greet(axis, [2 * p + core for p in order] + [partner])
    order = order + [place]
    pairs, copies = [], []
    for k, p in enumerate(order):
        copy = remote(x.at[2 * p + 1 - core], theirs.at[k], pair_send.at[k], pair_recv.at[k], axis, partner)
        copy.start()
        pairs.append(copy)
    for k, p in enumerate(order):
        pairs[k].wait_recv()
        total = x[2 * p + core] + theirs[k]
        if k < half - 1:
            leaving[k] = total.astype(leaving.dtype)
            copy = remote(leaving.at[k], landed.at[k], send.at[k], recv.at[k], axis, 2 * p + core)
            copy.start()
            copies.append(copy)
    for k, copy in enumerate(copies):
        copy.wait_recv()
        total = total + landed[k].astype(total.dtype)
    out[...] = total
    for copy in pairs + copies:
        copy.wait_send()


def pair_scatter(axis, x, collective_id):
    n = lax.axis_size(axis)
    half = n // 2
    block = x.shape[1:]
    dma = pltpu.SemaphoreType.DMA
    return call(
        functools.partial(pair_scatter_body, axis, n),
        [x], [jax.ShapeDtypeStruct(block, x.dtype)],
        [
            pltpu.VMEM((half, *block), x.dtype),
            pltpu.VMEM((half - 1, *block), jnp.bfloat16),
            pltpu.VMEM((half - 1, *block), jnp.bfloat16),
            dma((half - 1,)), dma((half - 1,)), dma((half,)), dma((half,)),
        ],
        collective_id,
    )[0]


def turned(axis, k):
    n = lax.axis_size(axis)
    return [(i, (i + k) % n) for i in range(n)]


def gather_turned(x, axis):
    return [x] + [lax.ppermute(x, axis, turned(axis, k)) for k in range(1, lax.axis_size(axis))]


def scatter_turned(x, axis):
    n, me = lax.axis_size(axis), lax.axis_index(axis)
    rows = x.shape[0] // n

    def part(k):
        return lax.dynamic_slice_in_dim(x, lax.rem(me + k, n) * rows, rows, 0)

    return [part(0)] + [lax.ppermute(part(k), axis, turned(axis, k)) for k in range(1, n)]


def lanes(rows):
    x = jnp.stack([r.astype(jnp.float32) for r in rows])
    return jnp.pad(x, ((0, -x.shape[0] % 8), (0, -x.shape[1] % 128)))


def shards(hidden, targets, loss_weight, head_weight, cluster_weight, tail_proj, tail_out):
    vocab_index = lax.axis_index("vocab")
    n_dp = lax.axis_size("dp")
    n_vocab = lax.axis_size("vocab")
    local, model = hidden.shape
    span = local * n_vocab
    share = model // n_dp
    cap = CLUSTER_TOKEN_CAP
    f32, bf16 = jnp.float32, jnp.bfloat16

    held, facts = pair_gather(
        "vocab", [hidden.reshape(2 * local, model // 2), lanes([targets, loss_weight])], 1
    )
    rows_hidden = held.reshape(span, model)
    row_targets = facts[:, 0, :local].reshape(span).astype(jnp.int32)
    gain_rows = facts[:, 1, :local].reshape(span)

    offset = row_targets - HEAD
    member = (offset >= 0) & (offset // CV == vocab_index)
    place = jnp.arange(span, dtype=jnp.int32)
    rank = jnp.sum((member[None, :] & (place[None, :] < place[:, None])).astype(jnp.int32), axis=1)
    slots = jnp.arange(cap, dtype=jnp.int32)
    own_select = member[None, :] & (rank[None, :] == slots[:, None])
    own_words = jnp.sum(jnp.where(own_select, offset[None, :] % CV, 0), axis=1).astype(jnp.int32)
    own_gains = jnp.sum(jnp.where(own_select, gain_rows[None, :], 0.0), axis=1)
    own_rows = jnp.dot(own_select.astype(bf16), rows_hidden, preferred_element_type=f32).astype(bf16)
    (tail_rows,) = exchange("dp", [own_rows], [], 2)
    tail_rows = tail_rows.reshape(n_dp * cap, model)

    proj = tail_proj[0]
    out = tail_out[0]
    reduced = jnp.dot(tail_rows, proj, preferred_element_type=f32).astype(bf16)
    partial_logits = jnp.dot(reduced, out, preferred_element_type=f32)

    rows_hidden, partial_logits = lax.optimization_barrier((rows_hidden, partial_logits))
    logit_parts = scatter_turned(partial_logits, "dp")

    local_logits = jnp.dot(rows_hidden, head_weight, preferred_element_type=f32)
    cluster_logit = jnp.dot(rows_hidden, cluster_weight, preferred_element_type=f32)
    width = head_weight.shape[1]
    columns = vocab_index * width + jnp.arange(width, dtype=jnp.int32)
    row_offset = row_targets - HEAD
    target_column = jnp.where(row_offset >= 0, HEAD + row_offset // CV, row_targets)
    top = jnp.maximum(jnp.max(local_logits, axis=1), cluster_logit[:, 0])
    total = jnp.sum(jnp.exp(local_logits - top[:, None]), axis=1) + jnp.exp(cluster_logit[:, 0] - top)
    (stats,) = exchange("vocab", [lanes([top, total])], [], 3)
    tops, totals = stats[:, 0, :span], stats[:, 1, :span]
    top = jnp.max(tops, axis=0)
    total = jnp.sum(totals * jnp.exp(tops - top[None, :]), axis=0)
    head_hot = (columns[None, :] == target_column[:, None]).astype(f32)
    head_delta = (
        gain_rows[:, None] * (jnp.exp(local_logits - top[:, None]) / total[:, None] - head_hot)
    ).astype(bf16)
    cluster_hot = (target_column == HEAD + vocab_index).astype(f32)[:, None]
    cluster_delta = (
        gain_rows[:, None] * (jnp.exp(cluster_logit - top[:, None]) / total[:, None] - cluster_hot)
    ).astype(bf16)
    token_partial = lax.dot_general(
        head_delta, head_weight, (((1,), (1,)), ((), ())), preferred_element_type=f32
    ) + cluster_delta.astype(f32) * cluster_weight.astype(f32).T

    deltas = jnp.concatenate([head_delta, cluster_delta], axis=1)
    deltas = jnp.pad(deltas, ((0, 0), (0, -deltas.shape[1] % 128)))
    deltas, behind, logit_parts = lax.optimization_barrier((deltas, rows_hidden, logit_parts))
    deltas = jnp.concatenate(gather_turned(deltas, "dp"))
    pieces = behind.reshape(span, n_dp, share).transpose(1, 0, 2).reshape(n_dp * span, share)
    hidden_columns = jnp.concatenate(scatter_turned(pieces, "dp"))

    word_logits = functools.reduce(jnp.add, logit_parts)
    word_top = jnp.max(word_logits, axis=1, keepdims=True)
    word_exp = jnp.exp(word_logits - word_top)
    word_prob = word_exp / jnp.sum(word_exp, axis=1, keepdims=True)
    word_columns = jnp.arange(word_logits.shape[1], dtype=jnp.int32)
    word_hot = (word_columns[None, :] == own_words[:, None]).astype(f32)
    own_word_delta = (own_gains[:, None] * (word_prob - word_hot)).astype(bf16)
    (word_delta,) = exchange("dp", [own_word_delta], [], 4)
    word_delta = word_delta.reshape(n_dp * cap, -1)
    all_delta, all_cluster_delta = deltas[:, :width], deltas[:, width : width + 1]
    reduced_grad = lax.dot_general(
        word_delta, out, (((1,), (1,)), ((), ())), preferred_element_type=f32
    ).astype(bf16)
    tail_partial = lax.dot_general(
        reduced_grad, proj, (((1,), (1,)), ((), ())), preferred_element_type=f32
    )
    tail_parts = scatter_turned(tail_partial.astype(bf16), "dp")
    tail_sum = functools.reduce(jnp.add, [part.astype(f32) for part in tail_parts]).astype(bf16)
    out_grad = lax.dot_general(
        reduced, word_delta, (((0,), (0,)), ((), ())), preferred_element_type=f32
    ).astype(bf16)
    proj_grad = lax.dot_general(
        tail_rows, reduced_grad, (((0,), (0,)), ((), ())), preferred_element_type=f32
    ).astype(bf16)

    head_grad = lax.dot_general(
        hidden_columns, all_delta, (((0,), (0,)), ((), ())), preferred_element_type=f32
    ).astype(bf16)
    cluster_grad = lax.dot_general(
        hidden_columns, all_cluster_delta, (((0,), (0,)), ((), ())), preferred_element_type=f32
    ).astype(bf16)

    spread_back = lax.dot_general(
        own_select.astype(bf16), tail_sum, (((0,), (0,)), ((), ())), preferred_element_type=f32
    )
    partial = (token_partial + spread_back).reshape(n_vocab, 2 * local, model // 2)
    hidden_grad = pair_scatter("vocab", partial, 6).reshape(local, model).astype(bf16)
    return (hidden_grad, head_grad, cluster_grad, proj_grad[None], out_grad[None])


def solution(mesh):
    placed = (
        P(("dp", "vocab"), None),
        P(("dp", "vocab")),
        P(("dp", "vocab")),
        P(None, "vocab"),
        P(None, "vocab"),
        P("vocab", None, "dp"),
        P("vocab", "dp", None),
    )
    return jax.shard_map(
        shards,
        mesh=mesh,
        in_specs=placed,
        out_specs=(
            P(("dp", "vocab"), None),
            P("dp", "vocab"),
            P("dp", "vocab"),
            P("vocab", None, "dp"),
            P("vocab", "dp", None),
        ),
        check_vma=False,
    )
```

```python
import functools

import jax
import jax.numpy as jnp
from jax import lax
from jax.experimental import pallas as pl
from jax.experimental.pallas import tpu as pltpu
from jax.sharding import PartitionSpec as P

HEAD = 10240
CV = 7680
CLUSTER_TOKEN_CAP = 16
MESH = pl.DeviceIdType.MESH
VMEM_LIMIT = 56 * 2**20


def remote(src, dst, send, recv, axis, peer):
    return pltpu.make_async_remote_copy(
        src_ref=src, dst_ref=dst, send_sem=send, recv_sem=recv,
        device_id={axis: peer}, device_id_type=MESH,
    )


def greet(*groups):
    barrier = pltpu.get_barrier_semaphore()
    for axis, peers in groups:
        for peer in peers:
            pl.semaphore_signal(barrier, inc=1, device_id={axis: peer}, device_id_type=MESH)
    pl.semaphore_wait(barrier, sum(len(peers) for _, peers in groups))


def call(body, operands, results, scratch, collective_id):
    vmem = pl.BlockSpec(memory_space=pltpu.VMEM)
    return pl.pallas_call(
        body,
        out_shape=results,
        in_specs=[vmem] * len(operands),
        out_specs=[vmem] * len(results),
        scratch_shapes=scratch,
        compiler_params=pltpu.CompilerParams(
            collective_id=collective_id, has_side_effects=True, vmem_limit_bytes=VMEM_LIMIT
        ),
    )(*operands)


def exchange_body(axis, n, split, count, *refs):
    ins, outs = refs[:count], refs[count : 2 * count]
    send, recv, local = refs[2 * count :]
    me = lax.axis_index(axis)
    peers = [lax.rem(me + k, n) for k in range(1, n)]
    greet((axis, peers))
    copies = []
    for i in range(count):
        for k, peer in enumerate(peers):
            src = ins[i].at[peer] if split[i] else ins[i]
            copy = remote(src, outs[i].at[me], send.at[i, k], recv.at[i, k], axis, peer)
            copy.start()
            copies.append(copy)
    for i in range(count):
        src = ins[i].at[me] if split[i] else ins[i]
        copy = pltpu.make_async_copy(src, outs[i].at[me], local.at[i])
        copy.start()
        copies.append(copy)
    for copy in copies:
        copy.wait()


def exchange(axis, gathers, splits, collective_id):
    n = lax.axis_size(axis)
    operands = [*gathers, *splits]
    count = len(operands)
    results = [jax.ShapeDtypeStruct((n, *a.shape), a.dtype) for a in gathers]
    results += [jax.ShapeDtypeStruct(a.shape, a.dtype) for a in splits]
    split = [False] * len(gathers) + [True] * len(splits)
    dma = pltpu.SemaphoreType.DMA
    return call(
        functools.partial(exchange_body, axis, n, split, count),
        operands, results,
        [dma((count, n - 1)), dma((count, n - 1)), dma((count,))],
        collective_id,
    )


def pair_gather_body(axis, n, count, *refs):
    ins, outs = refs[:count], refs[count : 2 * count]
    send, recv, pass_send, pass_recv, local = refs[2 * count :]
    half = n // 2
    me = lax.axis_index(axis)
    place, core = me // 2, lax.rem(me, 2)
    partner = 2 * place + 1 - core
    peers = [2 * lax.rem(place + k, half) + core for k in range(1, half)]
    greet((axis, peers + [partner]))
    copies, passed = [], []
    for i in range(count):
        for k, peer in enumerate(peers):
            copy = remote(ins[i], outs[i].at[me], send.at[i, k], recv.at[i, k], axis, peer)
            copy.start()
            copies.append(copy)
        copy = remote(ins[i], outs[i].at[me], pass_send.at[i, 0], pass_recv.at[i, 0], axis, partner)
        copy.start()
        passed.append(copy)
        copy = pltpu.make_async_copy(ins[i], outs[i].at[me], local.at[i])
        copy.start()
        passed.append(copy)
    for k in range(1, half):
        source = 2 * lax.rem(place + half - k, half) + core
        for i in range(count):
            copies[i * (half - 1) + k - 1].wait_recv()
            block = outs[i].at[source]
            copy = remote(block, block, pass_send.at[i, k], pass_recv.at[i, k], axis, partner)
            copy.start()
            passed.append(copy)
    for copy in copies:
        copy.wait_send()
    for copy in passed:
        copy.wait()


def pair_gather(axis, operands, collective_id):
    n = lax.axis_size(axis)
    count = len(operands)
    dma = pltpu.SemaphoreType.DMA
    half = n // 2
    return call(
        functools.partial(pair_gather_body, axis, n, count),
        operands,
        [jax.ShapeDtypeStruct((n, *a.shape), a.dtype) for a in operands],
        [dma((count, half - 1)), dma((count, half - 1)), dma((count, half)), dma((count, half)), dma((count,))],
        collective_id,
    )


def pair_scatter_body(
    axis, n, other, m, x, whole, parts, out, wholes, gathered,
    theirs, leaving, landed, send, recv, pair_send, pair_recv, far_send, far_recv, local,
):
    here = lax.axis_index(other)
    far = [lax.rem(here + k, m) for k in range(1, m)]
    half = n // 2
    me = lax.axis_index(axis)
    place, core = me // 2, lax.rem(me, 2)
    partner = 2 * place + 1 - core
    order = [lax.rem(place + k, half) for k in range(1, half)]
    greet((axis, [2 * p + core for p in order] + [partner]), (other, far))
    order = order + [place]
    pairs, copies, crossing = [], [], []
    for k, p in enumerate(order):
        copy = remote(x.at[2 * p + 1 - core], theirs.at[k], pair_send.at[k], pair_recv.at[k], axis, partner)
        copy.start()
        pairs.append(copy)
    for k, peer in enumerate(far):
        crossing += [
            remote(whole, wholes.at[here], far_send.at[0, k], far_recv.at[0, k], other, peer),
            remote(parts.at[peer], gathered.at[here], far_send.at[1, k], far_recv.at[1, k], other, peer),
        ]
    crossing += [
        pltpu.make_async_copy(whole, wholes.at[here], local.at[0]),
        pltpu.make_async_copy(parts.at[here], gathered.at[here], local.at[1]),
    ]
    for copy in crossing:
        copy.start()
    for k, p in enumerate(order):
        pairs[k].wait_recv()
        total = x[2 * p + core] + theirs[k]
        if k < half - 1:
            leaving[k] = total.astype(leaving.dtype)
            copy = remote(leaving.at[k], landed.at[k], send.at[k], recv.at[k], axis, 2 * p + core)
            copy.start()
            copies.append(copy)
    for k, copy in enumerate(copies):
        copy.wait_recv()
        total = total + landed[k].astype(total.dtype)
    out[...] = total
    for copy in pairs + copies:
        copy.wait_send()
    for copy in crossing:
        copy.wait()


def pair_scatter(axis, x, other, whole, parts, collective_id):
    n, m = lax.axis_size(axis), lax.axis_size(other)
    half = n // 2
    block = x.shape[1:]
    dma = pltpu.SemaphoreType.DMA
    return call(
        functools.partial(pair_scatter_body, axis, n, other, m),
        [x, whole, parts],
        [
            jax.ShapeDtypeStruct(block, x.dtype),
            jax.ShapeDtypeStruct((m, *whole.shape), whole.dtype),
            jax.ShapeDtypeStruct(parts.shape, parts.dtype),
        ],
        [
            pltpu.VMEM((half, *block), x.dtype),
            pltpu.VMEM((half - 1, *block), jnp.bfloat16),
            pltpu.VMEM((half - 1, *block), jnp.bfloat16),
            dma((half - 1,)), dma((half - 1,)), dma((half,)), dma((half,)),
            dma((2, m - 1)), dma((2, m - 1)), dma((2,)),
        ],
        collective_id,
    )


def turned(axis, k):
    n = lax.axis_size(axis)
    return [(i, (i + k) % n) for i in range(n)]


def scatter_turned(x, axis):
    n, me = lax.axis_size(axis), lax.axis_index(axis)
    rows = x.shape[0] // n

    def part(k):
        return lax.dynamic_slice_in_dim(x, lax.rem(me + k, n) * rows, rows, 0)

    return [part(0)] + [lax.ppermute(part(k), axis, turned(axis, k)) for k in range(1, n)]


def lanes(rows):
    x = jnp.stack([r.astype(jnp.float32) for r in rows])
    return jnp.pad(x, ((0, -x.shape[0] % 8), (0, -x.shape[1] % 128)))


def shards(hidden, targets, loss_weight, head_weight, cluster_weight, tail_proj, tail_out):
    vocab_index = lax.axis_index("vocab")
    n_dp = lax.axis_size("dp")
    n_vocab = lax.axis_size("vocab")
    local, model = hidden.shape
    span = local * n_vocab
    share = model // n_dp
    cap = CLUSTER_TOKEN_CAP
    f32, bf16 = jnp.float32, jnp.bfloat16

    held, facts = pair_gather(
        "vocab", [hidden.reshape(2 * local, model // 2), lanes([targets, loss_weight])], 1
    )
    rows_hidden = held.reshape(span, model)
    row_targets = facts[:, 0, :local].reshape(span).astype(jnp.int32)
    gain_rows = facts[:, 1, :local].reshape(span)

    offset = row_targets - HEAD
    member = (offset >= 0) & (offset // CV == vocab_index)
    place = jnp.arange(span, dtype=jnp.int32)
    rank = jnp.sum((member[None, :] & (place[None, :] < place[:, None])).astype(jnp.int32), axis=1)
    slots = jnp.arange(cap, dtype=jnp.int32)
    own_select = member[None, :] & (rank[None, :] == slots[:, None])
    own_words = jnp.sum(jnp.where(own_select, offset[None, :] % CV, 0), axis=1).astype(jnp.int32)
    own_gains = jnp.sum(jnp.where(own_select, gain_rows[None, :], 0.0), axis=1)
    own_rows = jnp.dot(own_select.astype(bf16), rows_hidden, preferred_element_type=f32).astype(bf16)
    (tail_rows,) = exchange("dp", [own_rows], [], 2)
    tail_rows = tail_rows.reshape(n_dp * cap, model)

    proj = tail_proj[0]
    out = tail_out[0]
    reduced = jnp.dot(tail_rows, proj, preferred_element_type=f32).astype(bf16)
    partial_logits = jnp.dot(reduced, out, preferred_element_type=f32)

    rows_hidden, partial_logits = lax.optimization_barrier((rows_hidden, partial_logits))
    logit_parts = scatter_turned(partial_logits, "dp")

    local_logits = jnp.dot(rows_hidden, head_weight, preferred_element_type=f32)
    cluster_logit = jnp.dot(rows_hidden, cluster_weight, preferred_element_type=f32)
    width = head_weight.shape[1]
    columns = vocab_index * width + jnp.arange(width, dtype=jnp.int32)
    row_offset = row_targets - HEAD
    target_column = jnp.where(row_offset >= 0, HEAD + row_offset // CV, row_targets)
    top = jnp.maximum(jnp.max(local_logits, axis=1), cluster_logit[:, 0])
    total = jnp.sum(jnp.exp(local_logits - top[:, None]), axis=1) + jnp.exp(cluster_logit[:, 0] - top)
    (stats,) = exchange("vocab", [lanes([top, total])], [], 3)
    tops, totals = stats[:, 0, :span], stats[:, 1, :span]
    top = jnp.max(tops, axis=0)
    total = jnp.sum(totals * jnp.exp(tops - top[None, :]), axis=0)
    head_hot = (columns[None, :] == target_column[:, None]).astype(f32)
    head_delta = (
        gain_rows[:, None] * (jnp.exp(local_logits - top[:, None]) / total[:, None] - head_hot)
    ).astype(bf16)
    cluster_hot = (target_column == HEAD + vocab_index).astype(f32)[:, None]
    cluster_delta = (
        gain_rows[:, None] * (jnp.exp(cluster_logit - top[:, None]) / total[:, None] - cluster_hot)
    ).astype(bf16)
    token_partial = lax.dot_general(
        head_delta, head_weight, (((1,), (1,)), ((), ())), preferred_element_type=f32
    ) + cluster_delta.astype(f32) * cluster_weight.astype(f32).T

    deltas = jnp.concatenate([head_delta, cluster_delta], axis=1)
    deltas = jnp.pad(deltas, ((0, 0), (0, -deltas.shape[1] % 128)))
    deltas, token_partial, logit_parts = lax.optimization_barrier((deltas, token_partial, logit_parts))
    pieces = rows_hidden.reshape(span, n_dp, share).transpose(1, 0, 2)

    word_logits = functools.reduce(jnp.add, logit_parts)
    word_top = jnp.max(word_logits, axis=1, keepdims=True)
    word_exp = jnp.exp(word_logits - word_top)
    word_prob = word_exp / jnp.sum(word_exp, axis=1, keepdims=True)
    word_columns = jnp.arange(word_logits.shape[1], dtype=jnp.int32)
    word_hot = (word_columns[None, :] == own_words[:, None]).astype(f32)
    own_word_delta = (own_gains[:, None] * (word_prob - word_hot)).astype(bf16)
    (word_delta,) = exchange("dp", [own_word_delta], [], 4)
    word_delta = word_delta.reshape(n_dp * cap, -1)
    reduced_grad = lax.dot_general(
        word_delta, out, (((1,), (1,)), ((), ())), preferred_element_type=f32
    ).astype(bf16)
    tail_partial = lax.dot_general(
        reduced_grad, proj, (((1,), (1,)), ((), ())), preferred_element_type=f32
    )
    tail_parts = scatter_turned(tail_partial.astype(bf16), "dp")
    tail_sum = functools.reduce(jnp.add, [part.astype(f32) for part in tail_parts]).astype(bf16)
    out_grad = lax.dot_general(
        reduced, word_delta, (((0,), (0,)), ((), ())), preferred_element_type=f32
    ).astype(bf16)
    proj_grad = lax.dot_general(
        tail_rows, reduced_grad, (((0,), (0,)), ((), ())), preferred_element_type=f32
    ).astype(bf16)

    spread_back = lax.dot_general(
        own_select.astype(bf16), tail_sum, (((0,), (0,)), ((), ())), preferred_element_type=f32
    )
    partial = (token_partial + spread_back).reshape(n_vocab, 2 * local, model // 2)
    hidden_grad, deltas, hidden_columns = pair_scatter("vocab", partial, "dp", deltas, pieces, 6)
    hidden_grad = hidden_grad.reshape(local, model).astype(bf16)
    deltas = deltas.reshape(n_dp * span, -1)
    hidden_columns = hidden_columns.reshape(n_dp * span, share)
    all_delta, all_cluster_delta = deltas[:, :width], deltas[:, width : width + 1]

    head_grad = lax.dot_general(
        hidden_columns, all_delta, (((0,), (0,)), ((), ())), preferred_element_type=f32
    ).astype(bf16)
    cluster_grad = lax.dot_general(
        hidden_columns, all_cluster_delta, (((0,), (0,)), ((), ())), preferred_element_type=f32
    ).astype(bf16)
    return (hidden_grad, head_grad, cluster_grad, proj_grad[None], out_grad[None])


def solution(mesh):
    placed = (
        P(("dp", "vocab"), None),
        P(("dp", "vocab")),
        P(("dp", "vocab")),
        P(None, "vocab"),
        P(None, "vocab"),
        P("vocab", None, "dp"),
        P("vocab", "dp", None),
    )
    return jax.shard_map(
        shards,
        mesh=mesh,
        in_specs=placed,
        out_specs=(
            P(("dp", "vocab"), None),
            P("dp", "vocab"),
            P("dp", "vocab"),
            P("vocab", None, "dp"),
            P("vocab", "dp", None),
        ),
        check_vma=False,
    )
```

```python
import functools

import jax
import jax.numpy as jnp
from jax import lax
from jax.experimental import pallas as pl
from jax.experimental.pallas import tpu as pltpu
from jax.sharding import PartitionSpec as P

HEAD = 10240
CV = 7680
CLUSTER_TOKEN_CAP = 16
MESH = pl.DeviceIdType.MESH
VMEM_LIMIT = 56 * 2**20


def remote(src, dst, send, recv, axis, peer):
    return pltpu.make_async_remote_copy(
        src_ref=src, dst_ref=dst, send_sem=send, recv_sem=recv,
        device_id={axis: peer}, device_id_type=MESH,
    )


def greet(*groups):
    barrier = pltpu.get_barrier_semaphore()
    for axis, peers in groups:
        for peer in peers:
            pl.semaphore_signal(barrier, inc=1, device_id={axis: peer}, device_id_type=MESH)
    pl.semaphore_wait(barrier, sum(len(peers) for _, peers in groups))


def call(body, operands, results, scratch, collective_id):
    vmem = pl.BlockSpec(memory_space=pltpu.VMEM)
    return pl.pallas_call(
        body,
        out_shape=results,
        in_specs=[vmem] * len(operands),
        out_specs=[vmem] * len(results),
        scratch_shapes=scratch,
        compiler_params=pltpu.CompilerParams(
            collective_id=collective_id, has_side_effects=True, vmem_limit_bytes=VMEM_LIMIT
        ),
    )(*operands)


def exchange_body(axis, n, split, count, *refs):
    ins, outs = refs[:count], refs[count : 2 * count]
    send, recv, local = refs[2 * count :]
    me = lax.axis_index(axis)
    peers = [lax.rem(me + k, n) for k in range(1, n)]
    greet((axis, peers))
    copies = []
    for i in range(count):
        for k, peer in enumerate(peers):
            src = ins[i].at[peer] if split[i] else ins[i]
            copy = remote(src, outs[i].at[me], send.at[i, k], recv.at[i, k], axis, peer)
            copy.start()
            copies.append(copy)
    for i in range(count):
        src = ins[i].at[me] if split[i] else ins[i]
        copy = pltpu.make_async_copy(src, outs[i].at[me], local.at[i])
        copy.start()
        copies.append(copy)
    for copy in copies:
        copy.wait()


def exchange(axis, gathers, splits, collective_id):
    n = lax.axis_size(axis)
    operands = [*gathers, *splits]
    count = len(operands)
    results = [jax.ShapeDtypeStruct((n, *a.shape), a.dtype) for a in gathers]
    results += [jax.ShapeDtypeStruct(a.shape, a.dtype) for a in splits]
    split = [False] * len(gathers) + [True] * len(splits)
    dma = pltpu.SemaphoreType.DMA
    return call(
        functools.partial(exchange_body, axis, n, split, count),
        operands, results,
        [dma((count, n - 1)), dma((count, n - 1)), dma((count,))],
        collective_id,
    )


def pair_gather_body(axis, n, count, *refs):
    ins, outs = refs[:count], refs[count : 2 * count]
    send, recv, pass_send, pass_recv, local = refs[2 * count :]
    half = n // 2
    me = lax.axis_index(axis)
    place, core = me // 2, lax.rem(me, 2)
    partner = 2 * place + 1 - core
    peers = [2 * lax.rem(place + k, half) + core for k in range(1, half)]
    greet((axis, peers + [partner]))
    copies, passed = [], []
    for i in range(count):
        for k, peer in enumerate(peers):
            copy = remote(ins[i], outs[i].at[me], send.at[i, k], recv.at[i, k], axis, peer)
            copy.start()
            copies.append(copy)
        copy = remote(ins[i], outs[i].at[me], pass_send.at[i, 0], pass_recv.at[i, 0], axis, partner)
        copy.start()
        passed.append(copy)
        copy = pltpu.make_async_copy(ins[i], outs[i].at[me], local.at[i])
        copy.start()
        passed.append(copy)
    for k in range(1, half):
        source = 2 * lax.rem(place + half - k, half) + core
        for i in range(count):
            copies[i * (half - 1) + k - 1].wait_recv()
            block = outs[i].at[source]
            copy = remote(block, block, pass_send.at[i, k], pass_recv.at[i, k], axis, partner)
            copy.start()
            passed.append(copy)
    for copy in copies:
        copy.wait_send()
    for copy in passed:
        copy.wait()


def pair_gather(axis, operands, collective_id):
    n = lax.axis_size(axis)
    count = len(operands)
    dma = pltpu.SemaphoreType.DMA
    half = n // 2
    return call(
        functools.partial(pair_gather_body, axis, n, count),
        operands,
        [jax.ShapeDtypeStruct((n, *a.shape), a.dtype) for a in operands],
        [dma((count, half - 1)), dma((count, half - 1)), dma((count, half)), dma((count, half)), dma((count,))],
        collective_id,
    )


def pair_scatter_body(
    axis, n, other, m, x, whole, out, wholes,
    theirs, leaving, landed, send, recv, pair_send, pair_recv, far_send, far_recv, local,
):
    here = lax.axis_index(other)
    far = [lax.rem(here + k, m) for k in range(1, m)]
    half = n // 2
    me = lax.axis_index(axis)
    place, core = me // 2, lax.rem(me, 2)
    partner = 2 * place + 1 - core
    order = [lax.rem(place + k, half) for k in range(1, half)]
    greet((axis, [2 * p + core for p in order] + [partner]), (other, far))
    order = order + [place]
    pairs, copies, crossing = [], [], []
    for k, p in enumerate(order):
        copy = remote(x.at[2 * p + 1 - core], theirs.at[k], pair_send.at[k], pair_recv.at[k], axis, partner)
        copy.start()
        pairs.append(copy)
    for k, peer in enumerate(far):
        crossing += [
            remote(whole, wholes.at[here], far_send.at[0, k], far_recv.at[0, k], other, peer),
        ]
    crossing += [
        pltpu.make_async_copy(whole, wholes.at[here], local.at[0]),
    ]
    for copy in crossing:
        copy.start()
    for k, p in enumerate(order):
        pairs[k].wait_recv()
        total = x[2 * p + core] + theirs[k]
        if k < half - 1:
            leaving[k] = total.astype(leaving.dtype)
            copy = remote(leaving.at[k], landed.at[k], send.at[k], recv.at[k], axis, 2 * p + core)
            copy.start()
            copies.append(copy)
    for k, copy in enumerate(copies):
        copy.wait_recv()
        total = total + landed[k].astype(total.dtype)
    out[...] = total
    for copy in pairs + copies:
        copy.wait_send()
    for copy in crossing:
        copy.wait()


def pair_scatter(axis, x, other, whole, collective_id):
    n, m = lax.axis_size(axis), lax.axis_size(other)
    half = n // 2
    block = x.shape[1:]
    dma = pltpu.SemaphoreType.DMA
    return call(
        functools.partial(pair_scatter_body, axis, n, other, m),
        [x, whole],
        [
            jax.ShapeDtypeStruct(block, x.dtype),
            jax.ShapeDtypeStruct((m, *whole.shape), whole.dtype),
        ],
        [
            pltpu.VMEM((half, *block), x.dtype),
            pltpu.VMEM((half - 1, *block), jnp.bfloat16),
            pltpu.VMEM((half - 1, *block), jnp.bfloat16),
            dma((half - 1,)), dma((half - 1,)), dma((half,)), dma((half,)),
            dma((1, m - 1)), dma((1, m - 1)), dma((1,)),
        ],
        collective_id,
    )


def turned(axis, k):
    n = lax.axis_size(axis)
    return [(i, (i + k) % n) for i in range(n)]


def scatter_turned(x, axis):
    n, me = lax.axis_size(axis), lax.axis_index(axis)
    rows = x.shape[0] // n

    def part(k):
        return lax.dynamic_slice_in_dim(x, lax.rem(me + k, n) * rows, rows, 0)

    return [part(0)] + [lax.ppermute(part(k), axis, turned(axis, k)) for k in range(1, n)]


def lanes(rows):
    x = jnp.stack([r.astype(jnp.float32) for r in rows])
    return jnp.pad(x, ((0, -x.shape[0] % 8), (0, -x.shape[1] % 128)))


def shards(hidden, targets, loss_weight, head_weight, cluster_weight, tail_proj, tail_out):
    vocab_index = lax.axis_index("vocab")
    n_dp = lax.axis_size("dp")
    n_vocab = lax.axis_size("vocab")
    local, model = hidden.shape
    span = local * n_vocab
    share = model // n_dp
    cap = CLUSTER_TOKEN_CAP
    f32, bf16 = jnp.float32, jnp.bfloat16

    held, facts = pair_gather(
        "vocab", [hidden.reshape(2 * local, model // 2), lanes([targets, loss_weight])], 1
    )
    rows_hidden = held.reshape(span, model)
    row_targets = facts[:, 0, :local].reshape(span).astype(jnp.int32)
    gain_rows = facts[:, 1, :local].reshape(span)

    offset = row_targets - HEAD
    member = (offset >= 0) & (offset // CV == vocab_index)
    place = jnp.arange(span, dtype=jnp.int32)
    rank = jnp.sum((member[None, :] & (place[None, :] < place[:, None])).astype(jnp.int32), axis=1)
    slots = jnp.arange(cap, dtype=jnp.int32)
    own_select = member[None, :] & (rank[None, :] == slots[:, None])
    own_words = jnp.sum(jnp.where(own_select, offset[None, :] % CV, 0), axis=1).astype(jnp.int32)
    own_gains = jnp.sum(jnp.where(own_select, gain_rows[None, :], 0.0), axis=1)
    own_rows = jnp.dot(own_select.astype(bf16), rows_hidden, preferred_element_type=f32).astype(bf16)
    pieces = rows_hidden.reshape(span, n_dp, share).transpose(1, 0, 2)
    tail_rows, hidden_columns = exchange("dp", [own_rows], [pieces], 2)
    tail_rows = tail_rows.reshape(n_dp * cap, model)

    proj = tail_proj[0]
    out = tail_out[0]
    reduced = jnp.dot(tail_rows, proj, preferred_element_type=f32).astype(bf16)
    partial_logits = jnp.dot(reduced, out, preferred_element_type=f32)

    rows_hidden, partial_logits = lax.optimization_barrier((rows_hidden, partial_logits))
    logit_parts = scatter_turned(partial_logits, "dp")

    local_logits = jnp.dot(rows_hidden, head_weight, preferred_element_type=f32)
    cluster_logit = jnp.dot(rows_hidden, cluster_weight, preferred_element_type=f32)
    width = head_weight.shape[1]
    columns = vocab_index * width + jnp.arange(width, dtype=jnp.int32)
    row_offset = row_targets - HEAD
    target_column = jnp.where(row_offset >= 0, HEAD + row_offset // CV, row_targets)
    top = jnp.maximum(jnp.max(local_logits, axis=1), cluster_logit[:, 0])
    total = jnp.sum(jnp.exp(local_logits - top[:, None]), axis=1) + jnp.exp(cluster_logit[:, 0] - top)
    (stats,) = exchange("vocab", [lanes([top, total])], [], 3)
    tops, totals = stats[:, 0, :span], stats[:, 1, :span]
    top = jnp.max(tops, axis=0)
    total = jnp.sum(totals * jnp.exp(tops - top[None, :]), axis=0)
    head_hot = (columns[None, :] == target_column[:, None]).astype(f32)
    head_delta = (
        gain_rows[:, None] * (jnp.exp(local_logits - top[:, None]) / total[:, None] - head_hot)
    ).astype(bf16)
    cluster_hot = (target_column == HEAD + vocab_index).astype(f32)[:, None]
    cluster_delta = (
        gain_rows[:, None] * (jnp.exp(cluster_logit - top[:, None]) / total[:, None] - cluster_hot)
    ).astype(bf16)
    token_partial = lax.dot_general(
        head_delta, head_weight, (((1,), (1,)), ((), ())), preferred_element_type=f32
    ) + cluster_delta.astype(f32) * cluster_weight.astype(f32).T

    deltas = jnp.concatenate([head_delta, cluster_delta], axis=1)
    deltas = jnp.pad(deltas, ((0, 0), (0, -deltas.shape[1] % 128)))
    deltas, token_partial, logit_parts = lax.optimization_barrier((deltas, token_partial, logit_parts))

    word_logits = functools.reduce(jnp.add, logit_parts)
    word_top = jnp.max(word_logits, axis=1, keepdims=True)
    word_exp = jnp.exp(word_logits - word_top)
    word_prob = word_exp / jnp.sum(word_exp, axis=1, keepdims=True)
    word_columns = jnp.arange(word_logits.shape[1], dtype=jnp.int32)
    word_hot = (word_columns[None, :] == own_words[:, None]).astype(f32)
    own_word_delta = (own_gains[:, None] * (word_prob - word_hot)).astype(bf16)
    (word_delta,) = exchange("dp", [own_word_delta], [], 4)
    word_delta = word_delta.reshape(n_dp * cap, -1)
    reduced_grad = lax.dot_general(
        word_delta, out, (((1,), (1,)), ((), ())), preferred_element_type=f32
    ).astype(bf16)
    tail_partial = lax.dot_general(
        reduced_grad, proj, (((1,), (1,)), ((), ())), preferred_element_type=f32
    )
    tail_parts = scatter_turned(tail_partial.astype(bf16), "dp")
    tail_sum = functools.reduce(jnp.add, [part.astype(f32) for part in tail_parts]).astype(bf16)
    out_grad = lax.dot_general(
        reduced, word_delta, (((0,), (0,)), ((), ())), preferred_element_type=f32
    ).astype(bf16)
    proj_grad = lax.dot_general(
        tail_rows, reduced_grad, (((0,), (0,)), ((), ())), preferred_element_type=f32
    ).astype(bf16)

    spread_back = lax.dot_general(
        own_select.astype(bf16), tail_sum, (((0,), (0,)), ((), ())), preferred_element_type=f32
    )
    partial = (token_partial + spread_back).reshape(n_vocab, 2 * local, model // 2)
    hidden_grad, deltas = pair_scatter("vocab", partial, "dp", deltas, 6)
    hidden_grad = hidden_grad.reshape(local, model).astype(bf16)
    deltas = deltas.reshape(n_dp * span, -1)
    hidden_columns = hidden_columns.reshape(n_dp * span, share)
    all_delta, all_cluster_delta = deltas[:, :width], deltas[:, width : width + 1]

    head_grad = lax.dot_general(
        hidden_columns, all_delta, (((0,), (0,)), ((), ())), preferred_element_type=f32
    ).astype(bf16)
    cluster_grad = lax.dot_general(
        hidden_columns, all_cluster_delta, (((0,), (0,)), ((), ())), preferred_element_type=f32
    ).astype(bf16)
    return (hidden_grad, head_grad, cluster_grad, proj_grad[None], out_grad[None])


def solution(mesh):
    placed = (
        P(("dp", "vocab"), None),
        P(("dp", "vocab")),
        P(("dp", "vocab")),
        P(None, "vocab"),
        P(None, "vocab"),
        P("vocab", None, "dp"),
        P("vocab", "dp", None),
    )
    return jax.shard_map(
        shards,
        mesh=mesh,
        in_specs=placed,
        out_specs=(
            P(("dp", "vocab"), None),
            P("dp", "vocab"),
            P("dp", "vocab"),
            P("vocab", None, "dp"),
            P("vocab", "dp", None),
        ),
        check_vma=False,
    )
```
